256 devices in a mesh: inner: 32 (over x, z), outer: 8 (over y, core).
Axes of the slice: x: 4, y: 4, z: 8, core: 2. Of those that a mesh axis runs over, the one named last changes fastest.
Arguments:
- queries: bfloat16 [2, 4, 8192], P(None, None, ('inner', 'outer')), may hold values from -300 to 300
- keys: bfloat16 [4, 65536, 1024], P(None, ('inner', 'outer')), may hold values from -6 to 6
- values: bfloat16 [4, 65536, 1024], P(None, ('inner', 'outer')), may hold values from -6 to 6
- lengths: int32 [4], replicated, may hold values from 4096 to 65535, as said below
Outputs:
- attended: float32 [2, 4, 8192], P(None, None, ('inner', 'outer'))
The draws below stay inside these ranges and needn't reach their ends.
Inputs may be any that keep to these rules, and one draw needn't show every extreme that they name: `lengths`: the largest length, 65535, is taken by some request in every draw.
All inputs are finite; a program needn't handle non-finite values.
Results may differ from the reference program's by a relative error of at most 0.0026.
Values may be sent and summed in bfloat16 or wider, within the bound.
A program may use at most 192 MiB of HBM per device.

```python
import jax
import jax.numpy as jnp
from jax import lax

HEADS = 64
KV_HEADS = 8
HEAD_DIM = 128
REQ = 4
CTX_DEV = 256
CONTEXT = 65536
N_INNER = 32
N_OUTER = 8


def base_keys(key):
    return jnp.clip(jax.random.normal(jax.random.fold_in(key, 5), (REQ, CONTEXT, KV_HEADS * HEAD_DIM)), -6.0, 6.0)


def draw_keys(key, part):
    anchor = key
    result = base_keys(anchor)
    return result.astype(jnp.bfloat16)


def draw_queries(key, part):
    key = jax.random.fold_in(key, 2)
    result = jnp.clip(jax.random.normal(key, (2, REQ, HEADS * HEAD_DIM)), -6.0, 6.0)
    return result.astype(jnp.bfloat16)


def draw_lengths(key, part):
    key = jax.random.fold_in(key, 3)
    span_key, pick_key = jax.random.split(key)
    drawn = jax.random.randint(span_key, (REQ,), CONTEXT // 16, CONTEXT)
    chosen = jax.random.randint(pick_key, (), 0, REQ)
    return jnp.where(jnp.arange(REQ) == chosen, CONTEXT - 1, drawn).astype(jnp.int32)


def block_scale(own_key, dims, pieces, least, high):
    factor_of = 1.0
    for axis_at, blocks in pieces:
        steps = jax.random.uniform(jax.random.fold_in(jax.random.fold_in(own_key, 6), axis_at), (blocks,), jnp.float32, least / len(pieces), high / len(pieces))
        factor_of = factor_of * jnp.repeat(jnp.exp(steps), dims[axis_at] // blocks).reshape((-1,) + (1,) * (len(dims) - 1 - axis_at))
    return factor_of


def bell_draw(rng, extent, scale, reach, shards=(), kind=jnp.bfloat16):
    values = scale * jax.random.normal(rng, extent, jnp.float32)
    if shards:
        values = values * block_scale(rng, extent, shards, -0.22, 0.18)
    return jnp.clip(values, -reach, reach).astype(kind)


def setup_inputs(seed: int = 0) -> dict:
    arg_keys = jax.random.split(jax.random.key(seed), 5)
    queries = draw_queries(jax.random.fold_in(arg_keys[4], 71), 0)
    keys = draw_keys(jax.random.fold_in(arg_keys[4], 71), 0)
    values = bell_draw(arg_keys[2], (REQ, CONTEXT, KV_HEADS * HEAD_DIM), 1.0, 6.0, ((1, 256),))
    lengths = draw_lengths(jax.random.fold_in(arg_keys[4], 71), 0)
    return dict(queries=queries, keys=keys, values=values, lengths=lengths)


NEGATIVE = -1e30


def reference(queries, keys, values, lengths):
    blocks = N_INNER * N_OUTER
    per_group = HEADS // KV_HEADS
    scale = 1.0 / (HEAD_DIM ** 0.5)
    position = jnp.arange(CONTEXT, dtype=jnp.int32).reshape(blocks, CTX_DEV)

    def per_request(items):
        query_row, key_rows, value_rows, length = items
        query_heads = query_row.reshape(2, KV_HEADS, per_group, HEAD_DIM).astype(jnp.float32)
        key_heads = key_rows.reshape(blocks, CTX_DEV, KV_HEADS, HEAD_DIM).astype(jnp.float32)
        value_heads = value_rows.reshape(blocks, CTX_DEV, KV_HEADS, HEAD_DIM).astype(jnp.float32)
        scores = jnp.einsum("sgqd,ntgd->sgqnt", query_heads, key_heads) * scale
        limit = length + jnp.arange(2, dtype=jnp.int32)
        valid = (position[None, :, :] < limit[:, None, None])[:, None, None, :, :]
        top = jnp.max(jnp.where(valid, scores, NEGATIVE), axis=-1)
        weight = jnp.where(valid, jnp.exp(scores - top[..., None]), 0.0)
        total = jnp.sum(weight, axis=-1)
        weight_low = lax.optimization_barrier(weight.astype(jnp.bfloat16)).astype(jnp.float32)
        part = jnp.einsum("sgqnt,ntgd->sgqnd", weight_low, value_heads)
        highest = jnp.max(top, axis=-1)
        factor = jnp.exp(top - highest[..., None])
        numerator = jnp.sum(part * factor[..., None], axis=3)
        denominator = jnp.sum(total * factor, axis=-1)
        result = numerator / denominator[..., None]
        return result.reshape(2, HEADS * HEAD_DIM)

    stacked = lax.map(per_request, (jnp.transpose(queries, (1, 0, 2)), keys, values, lengths))
    return jnp.transpose(stacked, (1, 0, 2))
```

```python
import functools

import jax
import jax.numpy as jnp
from jax import lax
from jax.experimental import pallas as pl
from jax.experimental.pallas import tpu as pltpu
from jax.sharding import PartitionSpec as P

HEAD_DIM = 128
NEGATIVE = -1e30
MESH = pl.DeviceIdType.MESH
NX, NZ, NY = 4, 8, 4
CHIPS = NX * NZ * NY


def lane_blocks(shape):
    return lax.broadcasted_iota(jnp.int32, shape, len(shape) - 1) // 32


def block_transpose(rows, block):
    odd = block % 2 == 1
    pairs = list(rows)
    for a in (0, 2):
        low, high = rows[a], rows[a + 1]
        pairs[a] = jnp.where(odd, pltpu.roll(high, 32, 1), low)
        pairs[a + 1] = jnp.where(odd, high, pltpu.roll(low, 96, 1))
    upper = block >= 2
    out = list(pairs)
    for a in (0, 1):
        low, high = pairs[a], pairs[a + 2]
        out[a] = jnp.where(upper, pltpu.roll(high, 64, 1), low)
        out[a + 2] = jnp.where(upper, high, pltpu.roll(low, 64, 1))
    return out


def kernel(
    q_ref, len_ref, k_hbm, v_hbm, o_ref,
    keys, vals, gath, sbuf, rbuf, parts, load_sem, gs_sem, gr_sem, cs_sem, cr_sem, rs_sem, rr_sem,
):
    inner, outer = lax.axis_index("inner"), lax.axis_index("outer")
    x, z, y, core = inner // NZ, inner % NZ, outer // 2, outer % 2
    me = inner * NY + y
    other = 1 - core
    partner = (inner, y * 2 + other)

    loads = []
    for r in range(4):
        loads.append(pltpu.make_async_copy(k_hbm.at[r], keys.at[r], load_sem.at[r]))
        loads.append(pltpu.make_async_copy(v_hbm.at[r], vals.at[r], load_sem.at[4 + r]))

    xs = [lax.rem(x + i, NX) * NZ for i in range(NX)]
    zs = [lax.rem(z + i, NZ) for i in range(NZ)]
    ys = [lax.rem(y + i, NY) for i in range(NY)]
    peers = []
    for k in (4, 3, 5, 2, 6, 1, 7, 0):
        for i in (2, 1, 3, 0):
            for j in (2, 1, 3, 0):
                if i or j or k:
                    peers.append((xs[i] + zs[k], ys[j]))

    barrier = pltpu.get_barrier_semaphore()
    for pi, py in peers:
        pl.semaphore_signal(barrier, inc=1, device_id=(pi, py * 2 + core), device_id_type=MESH)
    pl.semaphore_signal(barrier, inc=1, device_id=partner, device_id_type=MESH)
    for load in loads:
        load.start()

    lane = lax.broadcasted_iota(jnp.int32, (1, 128), 1)
    spread = (lax.broadcasted_iota(jnp.int32, (32, 128), 0) == lax.broadcasted_iota(jnp.int32, (32, 128), 1) % 32)
    wide = jnp.dot(q_ref[...], spread.astype(jnp.bfloat16), preferred_element_type=jnp.float32)
    row = lax.broadcasted_iota(jnp.int32, (8, 128), 0)
    keep = row % 4 == lax.broadcasted_iota(jnp.int32, (8, 128), 1) // 32
    wide = jnp.where(keep, wide, 0.0)
    own = jnp.concatenate([jnp.sum(wide[4 * s:4 * s + 4], axis=0, keepdims=True) for s in range(2)], axis=0)
    gath[core, me] = own
    pl.semaphore_wait(barrier, CHIPS)

    for pi, py in peers:
        pltpu.make_async_remote_copy(
            src_ref=gath.at[core, me], dst_ref=gath.at[core, me], send_sem=gs_sem, recv_sem=gr_sem,
            device_id=(pi, py * 2 + core), device_id_type=MESH,
        ).start()
    all_but_one = gath.at[0, pl.ds(0, CHIPS - 1)]
    pltpu.make_async_copy(all_but_one, all_but_one, gr_sem).wait()
    swap = pltpu.make_async_remote_copy(
        src_ref=gath.at[core], dst_ref=gath.at[core], send_sem=cs_sem.at[0], recv_sem=cr_sem.at[0],
        device_id=partner, device_id_type=MESH,
    )
    swap.start()
    swap.wait_recv()
    for load in loads:
        load.wait()

    scale = 1.0 / HEAD_DIM**0.5
    block = lane_blocks((8, 128))
    first_half = lax.broadcasted_iota(jnp.int32, (8, 128), 1) % 32 < 16
    position = (inner * 8 + outer) * 256 + lax.broadcasted_iota(jnp.int32, (16, 256), 1)
    step = lax.broadcasted_iota(jnp.int32, (16, 256), 0) // 8
    grows = gath.reshape(2, CHIPS * 2, 128)
    srows = sbuf.reshape(2, CHIPS * 4, 128)
    for g in range(8):
        fronts = []
        for s in range(2):
            pieces = [grows[k % 2, pl.ds(g * 32 + (k // 2) * 2 + s, 8, stride=4), :] for k in range(4)]
            fronts.append(block_transpose(pieces, block))
        results, tops, totals = [], [], []
        for r in range(4):
            q = jnp.concatenate([fronts[0][r], fronts[1][r]], axis=0).astype(jnp.bfloat16)
            score = lax.dot_general(
                q, keys[r, :, g * 128:(g + 1) * 128], (((1,), (1,)), ((), ())), preferred_element_type=jnp.float32
            ) * scale
            valid = position < len_ref[r] + step
            score = jnp.where(valid, score, NEGATIVE)
            top = jnp.max(score, axis=1, keepdims=True)
            weight = jnp.where(valid, jnp.exp(score - top), 0.0)
            total = jnp.sum(weight, axis=1, keepdims=True)
            part = jnp.dot(
                weight.astype(jnp.bfloat16), vals[r, :, g * 128:(g + 1) * 128], preferred_element_type=jnp.float32
            )
            results.append(part)
            tops.append(top)
            totals.append(total)
        top_row = jnp.zeros((8, 128), jnp.float32)
        total_row = jnp.zeros((8, 128), jnp.float32)
        for r in range(4):
            here = block == r
            top_row = jnp.where(here, jnp.where(first_half, tops[r][:8], tops[r][8:]), top_row)
            total_row = jnp.where(here, jnp.where(first_half, totals[r][:8], totals[r][8:]), total_row)
        backs = [block_transpose([results[r][8 * s:8 * s + 8] for r in range(4)], block) for s in range(2)]
        for k in range(4):
            at = g * 64 + (k // 2) * 4
            for i, value in enumerate((backs[0][k], backs[1][k], top_row, total_row)):
                srows[k % 2, pl.ds(at + i, 8, stride=8), :] = value

    give = pltpu.make_async_remote_copy(
        src_ref=sbuf.at[other], dst_ref=parts, send_sem=cs_sem.at[1], recv_sem=cr_sem.at[1],
        device_id=partner, device_id_type=MESH,
    )
    give.start()
    give.wait_recv()

    half = lax.broadcasted_iota(jnp.int32, (CHIPS, 128), 1) % 32 < 16

    def widen(v, half):
        return jnp.where(half, v, pltpu.roll(v, 16, 1)), jnp.where(half, pltpu.roll(v, 112, 1), v)

    prows = parts.reshape(CHIPS * 4, 128)
    mine = [srows[core, pl.ds(i, CHIPS, stride=4), :] for i in range(4)]
    theirs = [prows[pl.ds(i, CHIPS, stride=4), :] for i in range(4)]
    high = jnp.maximum(mine[2], theirs[2])
    fm, ft = jnp.exp(mine[2] - high), jnp.exp(theirs[2] - high)
    wm, wt = widen(fm, half), widen(ft, half)
    for s in range(2):
        srows[core, pl.ds(s, CHIPS, stride=4), :] = mine[s] * wm[s] + theirs[s] * wt[s]
    srows[core, pl.ds(2, CHIPS, stride=4), :] = high
    srows[core, pl.ds(3, CHIPS, stride=4), :] = mine[3] * fm + theirs[3] * ft

    for pi, py in peers:
        pltpu.make_async_remote_copy(
            src_ref=sbuf.at[core, pi * NY + py], dst_ref=rbuf.at[me], send_sem=rs_sem, recv_sem=rr_sem,
            device_id=(pi, py * 2 + core), device_id_type=MESH,
        ).start()
    rbuf[me] = sbuf[core, me]
    all_but_one = rbuf.at[pl.ds(0, CHIPS - 1)]
    pltpu.make_async_copy(all_but_one, all_but_one, rr_sem).wait()

    rrows = rbuf.reshape(CHIPS * 4, 128)
    got = [rrows[pl.ds(i, CHIPS, stride=4), :] for i in range(4)]
    high = jnp.max(got[2], axis=0, keepdims=True)
    factor = jnp.exp(got[2] - high)
    total = jnp.sum(got[3] * factor, axis=0, keepdims=True)
    total = widen(jnp.broadcast_to(total, (8, 128)), first_half)
    wide = widen(factor, half)
    for s in range(2):
        o_ref[s:s + 1, :] = jnp.sum(got[s] * wide[s], axis=0, keepdims=True) / total[s][:1]

    gone = gath.at[0, pl.ds(0, CHIPS - 1)]
    pltpu.make_async_copy(gone, gone, gs_sem).wait()
    swap.wait_send()
    give.wait_send()
    gone = rbuf.at[pl.ds(0, CHIPS - 1)]
    pltpu.make_async_copy(gone, gone, rs_sem).wait()


def body(queries, keys, values, lengths):
    out = pl.pallas_call(
        kernel,
        out_shape=jax.ShapeDtypeStruct((2, 128), jnp.float32),
        in_specs=[
            pl.BlockSpec(memory_space=pltpu.VMEM),
            pl.BlockSpec(memory_space=pltpu.SMEM),
            pl.BlockSpec(memory_space=pl.ANY),
            pl.BlockSpec(memory_space=pl.ANY),
        ],
        out_specs=pl.BlockSpec(memory_space=pltpu.VMEM),
        scratch_shapes=[
            pltpu.VMEM((4, 256, 1024), jnp.bfloat16),
            pltpu.VMEM((4, 256, 1024), jnp.bfloat16),
            pltpu.VMEM((2, CHIPS, 2, 128), jnp.float32),
            pltpu.VMEM((2, CHIPS, 4, 128), jnp.float32),
            pltpu.VMEM((CHIPS, 4, 128), jnp.float32),
            pltpu.VMEM((CHIPS, 4, 128), jnp.float32),
            pltpu.SemaphoreType.DMA((8,)),
            pltpu.SemaphoreType.DMA,
            pltpu.SemaphoreType.DMA,
            pltpu.SemaphoreType.DMA((2,)),
            pltpu.SemaphoreType.DMA((2,)),
            pltpu.SemaphoreType.DMA,
            pltpu.SemaphoreType.DMA,
        ],
        compiler_params=pltpu.CompilerParams(
            collective_id=0, has_side_effects=True, vmem_limit_bytes=24 << 20
        ),
        cost_estimate=pl.CostEstimate(flops=67108864, bytes_accessed=4 << 20, transcendentals=131072),
    )(queries.reshape(8, 32), lengths, keys, values)
    return out.reshape(2, 4, 32)


def solution(mesh):
    in_specs = (
        P(None, None, ("inner", "outer")),
        P(None, ("inner", "outer"), None),
        P(None, ("inner", "outer"), None),
        P(),
    )
    out_specs = P(None, None, ("inner", "outer"))
    return jax.shard_map(body, mesh=mesh, in_specs=in_specs, out_specs=out_specs, check_vma=False)
```

```python
import functools

import jax
import jax.numpy as jnp
from jax import lax
from jax.experimental import pallas as pl
from jax.experimental.pallas import tpu as pltpu
from jax.sharding import PartitionSpec as P

HEAD_DIM = 128
NEGATIVE = -1e30
MESH = pl.DeviceIdType.MESH
NX, NZ, NY = 4, 8, 4
CHIPS = NX * NZ * NY


def lane_blocks(shape):
    return lax.broadcasted_iota(jnp.int32, shape, len(shape) - 1) // 32


def block_transpose(rows, block):
    odd = block % 2 == 1
    pairs = list(rows)
    for a in (0, 2):
        low, high = rows[a], rows[a + 1]
        pairs[a] = jnp.where(odd, pltpu.roll(high, 32, 1), low)
        pairs[a + 1] = jnp.where(odd, high, pltpu.roll(low, 96, 1))
    upper = block >= 2
    out = list(pairs)
    for a in (0, 1):
        low, high = pairs[a], pairs[a + 2]
        out[a] = jnp.where(upper, pltpu.roll(high, 64, 1), low)
        out[a + 2] = jnp.where(upper, high, pltpu.roll(low, 64, 1))
    return out


def kernel(
    q_hbm, len_hbm, k_hbm, v_hbm, o_ref,
    q_ref, len_ref, small_sem, keys, vals, gath, sbuf, rbuf, parts, load_sem, gs_sem, gr_sem, cs_sem, cr_sem, rs_sem, rr_sem,
):
    inner, outer = lax.axis_index("inner"), lax.axis_index("outer")
    x, z, y, core = inner // NZ, inner % NZ, outer // 2, outer % 2
    me = inner * NY + y
    other = 1 - core
    partner = (inner, y * 2 + other)

    q_load = pltpu.make_async_copy(q_hbm, q_ref, small_sem.at[0])
    q_load.start()
    len_load = pltpu.make_async_copy(len_hbm, len_ref, small_sem.at[1])
    len_load.start()
    loads = []
    for r in range(4):
        loads.append(pltpu.make_async_copy(k_hbm.at[r], keys.at[r], load_sem.at[r]))
        loads.append(pltpu.make_async_copy(v_hbm.at[r], vals.at[r], load_sem.at[4 + r]))

    xs = [lax.rem(x + i, NX) * NZ for i in range(NX)]
    zs = [lax.rem(z + i, NZ) for i in range(NZ)]
    ys = [lax.rem(y + i, NY) for i in range(NY)]
    peers = []
    for k in (4, 3, 5, 2, 6, 1, 7, 0):
        for i in (2, 1, 3, 0):
            for j in (2, 1, 3, 0):
                if i or j or k:
                    peers.append((xs[i] + zs[k], ys[j]))

    barrier = pltpu.get_barrier_semaphore()
    for pi, py in peers:
        pl.semaphore_signal(barrier, inc=1, device_id=(pi, py * 2 + core), device_id_type=MESH)
    pl.semaphore_signal(barrier, inc=1, device_id=partner, device_id_type=MESH)
    for load in loads:
        load.start()

    lane = lax.broadcasted_iota(jnp.int32, (1, 128), 1)
    spread = (lax.broadcasted_iota(jnp.int32, (32, 128), 0) == lax.broadcasted_iota(jnp.int32, (32, 128), 1) % 32)
    q_load.wait()
    len_load.wait()
    wide = jnp.dot(q_ref[...], spread.astype(jnp.bfloat16), preferred_element_type=jnp.float32)
    row = lax.broadcasted_iota(jnp.int32, (8, 128), 0)
    keep = row % 4 == lax.broadcasted_iota(jnp.int32, (8, 128), 1) // 32
    wide = jnp.where(keep, wide, 0.0)
    own = jnp.concatenate([jnp.sum(wide[4 * s:4 * s + 4], axis=0, keepdims=True) for s in range(2)], axis=0)
    gath[core, me] = own
    pl.semaphore_wait(barrier, CHIPS)

    for pi, py in peers:
        pltpu.make_async_remote_copy(
            src_ref=gath.at[core, me], dst_ref=gath.at[core, me], send_sem=gs_sem, recv_sem=gr_sem,
            device_id=(pi, py * 2 + core), device_id_type=MESH,
        ).start()
    all_but_one = gath.at[0, pl.ds(0, CHIPS - 1)]
    pltpu.make_async_copy(all_but_one, all_but_one, gr_sem).wait()
    swap = pltpu.make_async_remote_copy(
        src_ref=gath.at[core], dst_ref=gath.at[core], send_sem=cs_sem.at[0], recv_sem=cr_sem.at[0],
        device_id=partner, device_id_type=MESH,
    )
    swap.start()
    swap.wait_recv()
    for load in loads:
        load.wait()

    scale = 1.0 / HEAD_DIM**0.5
    block = lane_blocks((8, 128))
    first_half = lax.broadcasted_iota(jnp.int32, (8, 128), 1) % 32 < 16
    grows = gath.reshape(2, CHIPS * 2, 128)
    srows = sbuf.reshape(2, CHIPS * 4, 128)
    fronts = []
    for g in range(8):
        pair = []
        for s in range(2):
            pieces = [grows[k % 2, pl.ds(g * 32 + (k // 2) * 2 + s, 8, stride=4), :] for k in range(4)]
            pair.append(block_transpose(pieces, block))
        fronts.append([jnp.concatenate([pair[0][r], pair[1][r]], axis=0).astype(jnp.bfloat16) for r in range(4)])

    position = (inner * 8 + outer) * 256 + lax.broadcasted_iota(jnp.int32, (256, 128), 0)
    step = lax.broadcasted_iota(jnp.int32, (256, 128), 1) // 8 % 2
    early = position - step
    blank = jnp.zeros((16, 128), jnp.bfloat16)
    results = [[None] * 4 for _ in range(8)]
    tops, totals = [], []
    for r in range(4):
        diagonal = jnp.concatenate(
            [jnp.concatenate([fronts[g][r] if a == g else blank for a in range(8)], axis=1) for g in range(8)], axis=0
        )
        score = lax.dot_general(
            keys[r], diagonal, (((1,), (1,)), ((), ())), preferred_element_type=jnp.float32
        ) * scale
        valid = early < len_ref[r]
        score = jnp.where(valid, score, NEGATIVE)
        top = jnp.max(score, axis=0, keepdims=True)
        weight = jnp.where(valid, jnp.exp(score - top), 0.0)
        tops.append(jnp.broadcast_to(top, (32, 128)))
        totals.append(jnp.broadcast_to(jnp.sum(weight, axis=0, keepdims=True), (32, 128)))
        turned = jnp.transpose(weight).astype(jnp.bfloat16)
        for a in range(4):
            part = jnp.dot(
                turned[32 * a:32 * a + 32], vals[r, :, 256 * a:256 * a + 256], preferred_element_type=jnp.float32
            )
            results[2 * a][r] = part[:16, :128]
            results[2 * a + 1][r] = part[16:, 128:]
    top_cols = jnp.transpose(jnp.concatenate(tops, axis=0))
    total_cols = jnp.transpose(jnp.concatenate(totals, axis=0))
    for g in range(8):
        top_row = jnp.where(first_half, top_cols[16 * g:16 * g + 8], top_cols[16 * g + 8:16 * g + 16])
        total_row = jnp.where(first_half, total_cols[16 * g:16 * g + 8], total_cols[16 * g + 8:16 * g + 16])
        backs = [block_transpose([results[g][r][8 * s:8 * s + 8] for r in range(4)], block) for s in range(2)]
        for k in range(4):
            at = g * 64 + (k // 2) * 4
            for i, value in enumerate((backs[0][k], backs[1][k], top_row, total_row)):
                srows[k % 2, pl.ds(at + i, 8, stride=8), :] = value

    give = pltpu.make_async_remote_copy(
        src_ref=sbuf.at[other], dst_ref=parts, send_sem=cs_sem.at[1], recv_sem=cr_sem.at[1],
        device_id=partner, device_id_type=MESH,
    )
    give.start()
    give.wait_recv()

    half = lax.broadcasted_iota(jnp.int32, (CHIPS, 128), 1) % 32 < 16

    def widen(v, half):
        return jnp.where(half, v, pltpu.roll(v, 16, 1)), jnp.where(half, pltpu.roll(v, 112, 1), v)

    prows = parts.reshape(CHIPS * 4, 128)
    mine = [srows[core, pl.ds(i, CHIPS, stride=4), :] for i in range(4)]
    theirs = [prows[pl.ds(i, CHIPS, stride=4), :] for i in range(4)]
    high = jnp.maximum(mine[2], theirs[2])
    fm, ft = jnp.exp(mine[2] - high), jnp.exp(theirs[2] - high)
    wm, wt = widen(fm, half), widen(ft, half)
    for s in range(2):
        srows[core, pl.ds(s, CHIPS, stride=4), :] = mine[s] * wm[s] + theirs[s] * wt[s]
    srows[core, pl.ds(2, CHIPS, stride=4), :] = high
    srows[core, pl.ds(3, CHIPS, stride=4), :] = mine[3] * fm + theirs[3] * ft

    for pi, py in peers:
        pltpu.make_async_remote_copy(
            src_ref=sbuf.at[core, pi * NY + py], dst_ref=rbuf.at[me], send_sem=rs_sem, recv_sem=rr_sem,
            device_id=(pi, py * 2 + core), device_id_type=MESH,
        ).start()
    rbuf[me] = sbuf[core, me]
    all_but_one = rbuf.at[pl.ds(0, CHIPS - 1)]
    pltpu.make_async_copy(all_but_one, all_but_one, rr_sem).wait()

    rrows = rbuf.reshape(CHIPS * 4, 128)
    got = [rrows[pl.ds(i, CHIPS, stride=4), :] for i in range(4)]
    high = jnp.max(got[2], axis=0, keepdims=True)
    factor = jnp.exp(got[2] - high)
    total = jnp.sum(got[3] * factor, axis=0, keepdims=True)
    total = widen(jnp.broadcast_to(total, (8, 128)), first_half)
    wide = widen(factor, half)
    for s in range(2):
        o_ref[s:s + 1, :] = jnp.sum(got[s] * wide[s], axis=0, keepdims=True) / total[s][:1]

    gone = gath.at[0, pl.ds(0, CHIPS - 1)]
    pltpu.make_async_copy(gone, gone, gs_sem).wait()
    swap.wait_send()
    give.wait_send()
    gone = rbuf.at[pl.ds(0, CHIPS - 1)]
    pltpu.make_async_copy(gone, gone, rs_sem).wait()


def body(queries, keys, values, lengths):
    out = pl.pallas_call(
        kernel,
        out_shape=jax.ShapeDtypeStruct((2, 128), jnp.float32),
        in_specs=[
            pl.BlockSpec(memory_space=pltpu.HBM),
            pl.BlockSpec(memory_space=pltpu.HBM),
            pl.BlockSpec(memory_space=pltpu.HBM),
            pl.BlockSpec(memory_space=pltpu.HBM),
        ],
        out_specs=pl.BlockSpec(memory_space=pltpu.VMEM),
        scratch_shapes=[
            pltpu.VMEM((8, 32), jnp.bfloat16),
            pltpu.SMEM((4,), jnp.int32),
            pltpu.SemaphoreType.DMA((2,)),
            pltpu.VMEM((4, 256, 1024), jnp.bfloat16),
            pltpu.VMEM((4, 256, 1024), jnp.bfloat16),
            pltpu.VMEM((2, CHIPS, 2, 128), jnp.float32),
            pltpu.VMEM((2, CHIPS, 4, 128), jnp.float32),
            pltpu.VMEM((CHIPS, 4, 128), jnp.float32),
            pltpu.VMEM((CHIPS, 4, 128), jnp.float32),
            pltpu.SemaphoreType.DMA((8,)),
            pltpu.SemaphoreType.DMA,
            pltpu.SemaphoreType.DMA,
            pltpu.SemaphoreType.DMA((2,)),
            pltpu.SemaphoreType.DMA((2,)),
            pltpu.SemaphoreType.DMA,
            pltpu.SemaphoreType.DMA,
        ],
        compiler_params=pltpu.CompilerParams(
            collective_id=0, has_side_effects=True, vmem_limit_bytes=60 << 20
        ),
        cost_estimate=pl.CostEstimate(flops=67108864, bytes_accessed=4 << 20, transcendentals=131072),
    )(queries.reshape(8, 32), lengths, keys, values)
    return out.reshape(2, 4, 32)


def solution(mesh):
    in_specs = (
        P(None, None, ("inner", "outer")),
        P(None, ("inner", "outer"), None),
        P(None, ("inner", "outer"), None),
        P(),
    )
    out_specs = P(None, None, ("inner", "outer"))
    return jax.shard_map(body, mesh=mesh, in_specs=in_specs, out_specs=out_specs, check_vma=False)
```

```python
import functools

import jax
import jax.numpy as jnp
from jax import lax
from jax.experimental import pallas as pl
from jax.experimental.pallas import tpu as pltpu
from jax.sharding import PartitionSpec as P

HEAD_DIM = 128
NEGATIVE = -1e30
MESH = pl.DeviceIdType.MESH
NX, NZ, NY = 4, 8, 4
CHIPS = NX * NZ * NY


def lane_blocks(shape):
    return lax.broadcasted_iota(jnp.int32, shape, len(shape) - 1) // 32


def block_transpose(rows, block):
    odd = block % 2 == 1
    pairs = list(rows)
    for a in (0, 2):
        low, high = rows[a], rows[a + 1]
        pairs[a] = jnp.where(odd, pltpu.roll(high, 32, 1), low)
        pairs[a + 1] = jnp.where(odd, high, pltpu.roll(low, 96, 1))
    upper = block >= 2
    out = list(pairs)
    for a in (0, 1):
        low, high = pairs[a], pairs[a + 2]
        out[a] = jnp.where(upper, pltpu.roll(high, 64, 1), low)
        out[a + 2] = jnp.where(upper, high, pltpu.roll(low, 64, 1))
    return out


def kernel(
    q_hbm, len_hbm, k_hbm, v_hbm, o_ref,
    q_ref, len_ref, small_sem, keys, vals, gath, sbuf, low, rbuf, wide, parts, load_sem, gs_sem, gr_sem, cs_sem, cr_sem, rs_sem, rr_sem,
):
    inner, outer = lax.axis_index("inner"), lax.axis_index("outer")
    x, z, y, core = inner // NZ, inner % NZ, outer // 2, outer % 2
    me = inner * NY + y
    other = 1 - core
    partner = (inner, y * 2 + other)

    q_load = pltpu.make_async_copy(q_hbm, q_ref, small_sem.at[0])
    q_load.start()
    len_load = pltpu.make_async_copy(len_hbm, len_ref, small_sem.at[1])
    len_load.start()
    loads = []
    for r in range(4):
        loads.append(pltpu.make_async_copy(k_hbm.at[r], keys.at[r], load_sem.at[r]))
        loads.append(pltpu.make_async_copy(v_hbm.at[r], vals.at[r], load_sem.at[4 + r]))

    xs = [lax.rem(x + i, NX) * NZ for i in range(NX)]
    zs = [lax.rem(z + i, NZ) for i in range(NZ)]
    ys = [lax.rem(y + i, NY) for i in range(NY)]
    peers = []
    for k in (4, 3, 5, 2, 6, 1, 7, 0):
        for i in (2, 1, 3, 0):
            for j in (2, 1, 3, 0):
                if i or j or k:
                    peers.append((xs[i] + zs[k], ys[j]))

    barrier = pltpu.get_barrier_semaphore()
    for pi, py in peers:
        pl.semaphore_signal(barrier, inc=1, device_id=(pi, py * 2 + core), device_id_type=MESH)
    pl.semaphore_signal(barrier, inc=1, device_id=partner, device_id_type=MESH)
    for load in loads:
        load.start()

    lane = lax.broadcasted_iota(jnp.int32, (1, 128), 1)
    spread = (lax.broadcasted_iota(jnp.int32, (32, 128), 0) == lax.broadcasted_iota(jnp.int32, (32, 128), 1) % 32)
    q_load.wait()
    len_load.wait()
    mine = jnp.dot(q_ref[...], spread.astype(jnp.bfloat16), preferred_element_type=jnp.float32)
    row = lax.broadcasted_iota(jnp.int32, (8, 128), 0)
    keep = row % 4 == lax.broadcasted_iota(jnp.int32, (8, 128), 1) // 32
    mine = jnp.where(keep, mine, 0.0)
    own = jnp.concatenate([jnp.sum(mine[4 * s:4 * s + 4], axis=0, keepdims=True) for s in range(2)], axis=0)
    gath[core, me] = own
    pl.semaphore_wait(barrier, CHIPS)

    for pi, py in peers:
        pltpu.make_async_remote_copy(
            src_ref=gath.at[core, me], dst_ref=gath.at[core, me], send_sem=gs_sem, recv_sem=gr_sem,
            device_id=(pi, py * 2 + core), device_id_type=MESH,
        ).start()
    all_but_one = gath.at[0, pl.ds(0, CHIPS - 1)]
    pltpu.make_async_copy(all_but_one, all_but_one, gr_sem).wait()
    swap = pltpu.make_async_remote_copy(
        src_ref=gath.at[core], dst_ref=gath.at[core], send_sem=cs_sem.at[0], recv_sem=cr_sem.at[0],
        device_id=partner, device_id_type=MESH,
    )
    swap.start()
    swap.wait_recv()
    for load in loads:
        load.wait()

    scale = 1.0 / HEAD_DIM**0.5
    block = lane_blocks((8, 128))
    first_half = lax.broadcasted_iota(jnp.int32, (8, 128), 1) % 32 < 16
    grows = gath.reshape(2, CHIPS * 2, 128)
    srows = sbuf.reshape(2, CHIPS * 4, 128)
    fronts = []
    for g in range(8):
        pair = []
        for s in range(2):
            pieces = [grows[k % 2, pl.ds(g * 32 + (k // 2) * 2 + s, 8, stride=4), :] for k in range(4)]
            pair.append(block_transpose(pieces, block))
        fronts.append([jnp.concatenate([pair[0][r], pair[1][r]], axis=0).astype(jnp.bfloat16) for r in range(4)])

    position = (inner * 8 + outer) * 256 + lax.broadcasted_iota(jnp.int32, (256, 128), 0)
    step = lax.broadcasted_iota(jnp.int32, (256, 128), 1) // 8 % 2
    early = position - step
    blank = jnp.zeros((16, 128), jnp.bfloat16)
    results = [[None] * 4 for _ in range(8)]
    tops, totals = [], []
    for r in range(4):
        diagonal = jnp.concatenate(
            [jnp.concatenate([fronts[g][r] if a == g else blank for a in range(8)], axis=1) for g in range(8)], axis=0
        )
        score = lax.dot_general(
            keys[r], diagonal, (((1,), (1,)), ((), ())), preferred_element_type=jnp.float32
        ) * scale
        valid = early < len_ref[r]
        score = jnp.where(valid, score, NEGATIVE)
        top = jnp.max(score, axis=0, keepdims=True)
        weight = jnp.where(valid, jnp.exp(score - top), 0.0)
        tops.append(jnp.broadcast_to(top, (32, 128)))
        totals.append(jnp.broadcast_to(jnp.sum(weight, axis=0, keepdims=True), (32, 128)))
        turned = jnp.transpose(weight).astype(jnp.bfloat16)
        for a in range(4):
            part = jnp.dot(
                turned[32 * a:32 * a + 32], vals[r, :, 256 * a:256 * a + 256], preferred_element_type=jnp.float32
            )
            results[2 * a][r] = part[:16, :128]
            results[2 * a + 1][r] = part[16:, 128:]
    top_cols = jnp.transpose(jnp.concatenate(tops, axis=0))
    total_cols = jnp.transpose(jnp.concatenate(totals, axis=0))
    for g in range(8):
        top_row = jnp.where(first_half, top_cols[16 * g:16 * g + 8], top_cols[16 * g + 8:16 * g + 16])
        total_row = jnp.where(first_half, total_cols[16 * g:16 * g + 8], total_cols[16 * g + 8:16 * g + 16])
        backs = [block_transpose([results[g][r][8 * s:8 * s + 8] for r in range(4)], block) for s in range(2)]
        for k in range(4):
            at = g * 64 + (k // 2) * 4
            for i, value in enumerate((backs[0][k], backs[1][k], top_row, total_row)):
                srows[k % 2, pl.ds(at + i, 8, stride=8), :] = value

    give = pltpu.make_async_remote_copy(
        src_ref=sbuf.at[other], dst_ref=parts, send_sem=cs_sem.at[1], recv_sem=cr_sem.at[1],
        device_id=partner, device_id_type=MESH,
    )
    give.start()
    give.wait_recv()

    tall = lax.broadcasted_iota(jnp.int32, (CHIPS, 128), 1)
    half = tall % 32 < 16

    def widen(v, half):
        return jnp.where(half, v, pltpu.roll(v, 16, 1)), jnp.where(half, pltpu.roll(v, 112, 1), v)

    def split(v):
        high = v.astype(jnp.bfloat16).astype(jnp.float32)
        rest = v - high
        middle = rest.astype(jnp.bfloat16).astype(jnp.float32)
        slot = tall % 16 // 4
        return jnp.where(slot == 0, high, jnp.where(slot == 1, middle, jnp.where(slot == 2, rest - middle, 0.0)))

    prows = parts.reshape(CHIPS * 4, 128)
    mine = [srows[core, pl.ds(i, CHIPS, stride=4), :] for i in range(4)]
    theirs = [prows[pl.ds(i, CHIPS, stride=4), :] for i in range(4)]
    high = jnp.maximum(mine[2], theirs[2])
    fm, ft = jnp.exp(mine[2] - high), jnp.exp(theirs[2] - high)
    wm, wt = widen(fm, half), widen(ft, half)
    for s in range(2):
        srows[core, pl.ds(s, CHIPS, stride=4), :] = mine[s] * wm[s] + theirs[s] * wt[s]
    srows[core, pl.ds(2, CHIPS, stride=4), :] = split(high)
    srows[core, pl.ds(3, CHIPS, stride=4), :] = split(mine[3] * fm + theirs[3] * ft)
    low.reshape(CHIPS * 4, 128)[...] = srows[core].astype(jnp.bfloat16)

    for pi, py in peers:
        pltpu.make_async_remote_copy(
            src_ref=low.at[pi * NY + py], dst_ref=rbuf.at[me], send_sem=rs_sem, recv_sem=rr_sem,
            device_id=(pi, py * 2 + core), device_id_type=MESH,
        ).start()
    rbuf[me] = low[me]
    source = lax.broadcasted_iota(jnp.int32, (128, 128), 0)
    target = lax.broadcasted_iota(jnp.int32, (128, 128), 1)
    same = source // 32 == target // 32
    gather_step = [(same & (source // 16 % 2 == s) & (source % 4 == 0)).astype(jnp.bfloat16) for s in range(2)]
    all_but_one = rbuf.at[pl.ds(0, CHIPS - 1)]
    pltpu.make_async_copy(all_but_one, all_but_one, rr_sem).wait()

    wide.reshape(CHIPS * 4, 128)[...] = rbuf.reshape(CHIPS * 4, 128)[...].astype(jnp.float32)
    wrows = wide.reshape(CHIPS * 4, 128)
    got = [wrows[pl.ds(i, CHIPS, stride=4), :] for i in range(4)]
    top_bits, total_bits = got[2].astype(jnp.bfloat16), got[3].astype(jnp.bfloat16)
    for s in range(2):
        top = jnp.dot(top_bits, gather_step[s], preferred_element_type=jnp.float32)
        total = jnp.dot(total_bits, gather_step[s], preferred_element_type=jnp.float32)
        factor = jnp.exp(top - jnp.max(top, axis=0, keepdims=True))
        o_ref[s:s + 1, :] = jnp.sum(got[s] * factor, axis=0, keepdims=True) / jnp.sum(
            total * factor, axis=0, keepdims=True
        )

    gone = gath.at[0, pl.ds(0, CHIPS - 1)]
    pltpu.make_async_copy(gone, gone, gs_sem).wait()
    swap.wait_send()
    give.wait_send()
    gone = rbuf.at[pl.ds(0, CHIPS - 1)]
    pltpu.make_async_copy(gone, gone, rs_sem).wait()


def body(queries, keys, values, lengths):
    out = pl.pallas_call(
        kernel,
        out_shape=jax.ShapeDtypeStruct((2, 128), jnp.float32),
        in_specs=[
            pl.BlockSpec(memory_space=pltpu.HBM),
            pl.BlockSpec(memory_space=pltpu.HBM),
            pl.BlockSpec(memory_space=pltpu.HBM),
            pl.BlockSpec(memory_space=pltpu.HBM),
        ],
        out_specs=pl.BlockSpec(memory_space=pltpu.VMEM),
        scratch_shapes=[
            pltpu.VMEM((8, 32), jnp.bfloat16),
            pltpu.SMEM((4,), jnp.int32),
            pltpu.SemaphoreType.DMA((2,)),
            pltpu.VMEM((4, 256, 1024), jnp.bfloat16),
            pltpu.VMEM((4, 256, 1024), jnp.bfloat16),
            pltpu.VMEM((2, CHIPS, 2, 128), jnp.float32),
            pltpu.VMEM((2, CHIPS, 4, 128), jnp.float32),
            pltpu.VMEM((CHIPS, 4, 128), jnp.bfloat16),
            pltpu.VMEM((CHIPS, 4, 128), jnp.bfloat16),
            pltpu.VMEM((CHIPS, 4, 128), jnp.float32),
            pltpu.VMEM((CHIPS, 4, 128), jnp.float32),
            pltpu.SemaphoreType.DMA((8,)),
            pltpu.SemaphoreType.DMA,
            pltpu.SemaphoreType.DMA,
            pltpu.SemaphoreType.DMA((2,)),
            pltpu.SemaphoreType.DMA((2,)),
            pltpu.SemaphoreType.DMA,
            pltpu.SemaphoreType.DMA,
        ],
        compiler_params=pltpu.CompilerParams(
            collective_id=0, has_side_effects=True, vmem_limit_bytes=60 << 20
        ),
        cost_estimate=pl.CostEstimate(flops=67108864, bytes_accessed=4 << 20, transcendentals=131072),
    )(queries.reshape(8, 32), lengths, keys, values)
    return out.reshape(2, 4, 32)


def solution(mesh):
    in_specs = (
        P(None, None, ("inner", "outer")),
        P(None, ("inner", "outer"), None),
        P(None, ("inner", "outer"), None),
        P(),
    )
    out_specs = P(None, None, ("inner", "outer"))
    return jax.shard_map(body, mesh=mesh, in_specs=in_specs, out_specs=out_specs, check_vma=False)
```

```python
import functools

import jax
import jax.numpy as jnp
from jax import lax
from jax.experimental import pallas as pl
from jax.experimental.pallas import tpu as pltpu
from jax.sharding import PartitionSpec as P

HEAD_DIM = 128
NEGATIVE = -1e30
MESH = pl.DeviceIdType.MESH
NX, NZ, NY = 4, 8, 4
CHIPS = NX * NZ * NY


def lane_blocks(shape):
    return lax.broadcasted_iota(jnp.int32, shape, len(shape) - 1) // 32


def block_transpose(rows, block):
    odd = block % 2 == 1
    pairs = list(rows)
    for a in (0, 2):
        low, high = rows[a], rows[a + 1]
        pairs[a] = jnp.where(odd, pltpu.roll(high, 32, 1), low)
        pairs[a + 1] = jnp.where(odd, high, pltpu.roll(low, 96, 1))
    upper = block >= 2
    out = list(pairs)
    for a in (0, 1):
        low, high = pairs[a], pairs[a + 2]
        out[a] = jnp.where(upper, pltpu.roll(high, 64, 1), low)
        out[a + 2] = jnp.where(upper, high, pltpu.roll(low, 64, 1))
    return out


def kernel(
    q_hbm, len_hbm, k_hbm, v_hbm, o_ref,
    q_ref, len_ref, small_sem, keys, vals, gath, sbuf, low, rbuf, wide, parts, load_sem, gs_sem, gr_sem, cs_sem, cr_sem, rs_sem, rr_sem,
):
    inner, outer = lax.axis_index("inner"), lax.axis_index("outer")
    x, z, y, core = inner // NZ, inner % NZ, outer // 2, outer % 2
    me = inner * NY + y
    other = 1 - core
    partner = (inner, y * 2 + other)

    q_load = pltpu.make_async_copy(q_hbm, q_ref, small_sem.at[0])
    q_load.start()
    len_load = pltpu.make_async_copy(len_hbm, len_ref, small_sem.at[1])
    len_load.start()
    loads = []
    for r in range(4):
        loads.append(pltpu.make_async_copy(k_hbm.at[r], keys.at[r], load_sem.at[r]))
        loads.append(pltpu.make_async_copy(v_hbm.at[r], vals.at[r], load_sem.at[4 + r]))

    xs = [lax.rem(x + i, NX) * NZ for i in range(NX)]
    zs = [lax.rem(z + i, NZ) for i in range(NZ)]
    ys = [lax.rem(y + i, NY) for i in range(NY)]
    peers = []
    for k in (4, 3, 5, 2, 6, 1, 7, 0):
        for i in (2, 1, 3, 0):
            for j in (2, 1, 3, 0):
                if i or j or k:
                    peers.append((xs[i] + zs[k], ys[j]))

    barrier = pltpu.get_barrier_semaphore()
    for pi, py in peers:
        pl.semaphore_signal(barrier, inc=1, device_id=(pi, py * 2 + core), device_id_type=MESH)
    pl.semaphore_signal(barrier, inc=1, device_id=partner, device_id_type=MESH)
    for load in loads:
        load.start()

    lane = lax.broadcasted_iota(jnp.int32, (1, 128), 1)
    spread = (lax.broadcasted_iota(jnp.int32, (32, 128), 0) == lax.broadcasted_iota(jnp.int32, (32, 128), 1) % 32)
    q_load.wait()
    len_load.wait()
    mine = jnp.dot(q_ref[...], spread.astype(jnp.bfloat16), preferred_element_type=jnp.float32)
    row = lax.broadcasted_iota(jnp.int32, (8, 128), 0)
    keep = row % 4 == lax.broadcasted_iota(jnp.int32, (8, 128), 1) // 32
    mine = jnp.where(keep, mine, 0.0)
    own = jnp.concatenate([jnp.sum(mine[4 * s:4 * s + 4], axis=0, keepdims=True) for s in range(2)], axis=0)
    gath[core, me] = own
    pl.semaphore_wait(barrier, CHIPS)

    for pi, py in peers:
        pltpu.make_async_remote_copy(
            src_ref=gath.at[core, me], dst_ref=gath.at[core, me], send_sem=gs_sem, recv_sem=gr_sem,
            device_id=(pi, py * 2 + core), device_id_type=MESH,
        ).start()
    all_but_one = gath.at[0, pl.ds(0, CHIPS - 1)]
    pltpu.make_async_copy(all_but_one, all_but_one, gr_sem).wait()
    swap = pltpu.make_async_remote_copy(
        src_ref=gath.at[core], dst_ref=gath.at[core], send_sem=cs_sem.at[0], recv_sem=cr_sem.at[0],
        device_id=partner, device_id_type=MESH,
    )
    swap.start()
    swap.wait_recv()
    for load in loads:
        load.wait()

    scale = 1.0 / HEAD_DIM**0.5
    block = lane_blocks((8, 128))
    first_half = lax.broadcasted_iota(jnp.int32, (8, 128), 1) % 32 < 16
    grows = gath.reshape(2, CHIPS * 2, 128)
    srows = sbuf.reshape(2, CHIPS * 4, 128)
    fronts = []
    for g in range(8):
        pair = []
        for s in range(2):
            pieces = [grows[k % 2, pl.ds(g * 32 + (k // 2) * 2 + s, 8, stride=4), :] for k in range(4)]
            pair.append(block_transpose(pieces, block))
        fronts.append([jnp.concatenate([pair[0][r], pair[1][r]], axis=0).astype(jnp.bfloat16) for r in range(4)])

    position = (inner * 8 + outer) * 256 + lax.broadcasted_iota(jnp.int32, (256, 128), 0)
    step = lax.broadcasted_iota(jnp.int32, (256, 128), 1) // 8 % 2
    early = position - step
    blank = jnp.zeros((16, 128), jnp.bfloat16)
    results = [[None] * 4 for _ in range(8)]
    tops, totals = [], []
    scores = []
    for r in range(4):
        diagonal = jnp.concatenate(
            [jnp.concatenate([fronts[g][r] if a == g else blank for a in range(8)], axis=1) for g in range(8)], axis=0
        )
        scores.append(lax.dot_general(
            keys[r], diagonal, (((1,), (1,)), ((), ())), preferred_element_type=jnp.float32
        ))
    turned = []
    for r in range(4):
        score = jnp.where(early < len_ref[r], scores[r] * scale, NEGATIVE)
        top = jnp.max(score, axis=0, keepdims=True)
        weight = jnp.exp(score - jnp.maximum(top, 0.5 * NEGATIVE))
        tops.append(jnp.broadcast_to(top, (32, 128)))
        totals.append(jnp.broadcast_to(jnp.sum(weight, axis=0, keepdims=True), (32, 128)))
        turned.append(jnp.transpose(weight).astype(jnp.bfloat16))
    for r in range(4):
        for a in range(4):
            part = jnp.dot(
                turned[r][32 * a:32 * a + 32], vals[r, :, 256 * a:256 * a + 256], preferred_element_type=jnp.float32
            )
            results[2 * a][r] = part[:16, :128]
            results[2 * a + 1][r] = part[16:, 128:]
    top_cols = jnp.transpose(jnp.concatenate(tops, axis=0))
    total_cols = jnp.transpose(jnp.concatenate(totals, axis=0))
    for g in range(8):
        top_row = jnp.where(first_half, top_cols[16 * g:16 * g + 8], top_cols[16 * g + 8:16 * g + 16])
        total_row = jnp.where(first_half, total_cols[16 * g:16 * g + 8], total_cols[16 * g + 8:16 * g + 16])
        backs = [block_transpose([results[g][r][8 * s:8 * s + 8] for r in range(4)], block) for s in range(2)]
        for k in range(4):
            at = g * 64 + (k // 2) * 4
            for i, value in enumerate((backs[0][k], backs[1][k], top_row, total_row)):
                srows[k % 2, pl.ds(at + i, 8, stride=8), :] = value

    give = pltpu.make_async_remote_copy(
        src_ref=sbuf.at[other], dst_ref=parts, send_sem=cs_sem.at[1], recv_sem=cr_sem.at[1],
        device_id=partner, device_id_type=MESH,
    )
    give.start()
    give.wait_recv()

    tall = lax.broadcasted_iota(jnp.int32, (CHIPS, 128), 1)
    half = tall % 32 < 16

    def widen(v, half):
        return jnp.where(half, v, pltpu.roll(v, 16, 1)), jnp.where(half, pltpu.roll(v, 112, 1), v)

    def split(v):
        high = v.astype(jnp.bfloat16).astype(jnp.float32)
        rest = v - high
        middle = rest.astype(jnp.bfloat16).astype(jnp.float32)
        slot = tall % 16 // 4
        return jnp.where(slot == 0, high, jnp.where(slot == 1, middle, jnp.where(slot == 2, rest - middle, 0.0)))

    prows = parts.reshape(CHIPS * 4, 128)
    mine = [srows[core, pl.ds(i, CHIPS, stride=4), :] for i in range(4)]
    theirs = [prows[pl.ds(i, CHIPS, stride=4), :] for i in range(4)]
    high = jnp.maximum(mine[2], theirs[2])
    fm, ft = jnp.exp(mine[2] - high), jnp.exp(theirs[2] - high)
    wm, wt = widen(fm, half), widen(ft, half)
    for s in range(2):
        srows[core, pl.ds(s, CHIPS, stride=4), :] = mine[s] * wm[s] + theirs[s] * wt[s]
    srows[core, pl.ds(2, CHIPS, stride=4), :] = split(high)
    srows[core, pl.ds(3, CHIPS, stride=4), :] = split(mine[3] * fm + theirs[3] * ft)
    low.reshape(CHIPS * 4, 128)[...] = srows[core].astype(jnp.bfloat16)

    for pi, py in peers:
        pltpu.make_async_remote_copy(
            src_ref=low.at[pi * NY + py], dst_ref=rbuf.at[me], send_sem=rs_sem, recv_sem=rr_sem,
            device_id=(pi, py * 2 + core), device_id_type=MESH,
        ).start()
    rbuf[me] = low[me]
    source = lax.broadcasted_iota(jnp.int32, (128, 128), 0)
    target = lax.broadcasted_iota(jnp.int32, (128, 128), 1)
    same = source // 32 == target // 32
    gather_step = [(same & (source // 16 % 2 == s) & (source % 4 == 0)).astype(jnp.bfloat16) for s in range(2)]
    all_but_one = rbuf.at[pl.ds(0, CHIPS - 1)]
    pltpu.make_async_copy(all_but_one, all_but_one, rr_sem).wait()

    wide.reshape(CHIPS * 4, 128)[...] = rbuf.reshape(CHIPS * 4, 128)[...].astype(jnp.float32)
    wrows = wide.reshape(CHIPS * 4, 128)
    got = [wrows[pl.ds(i, CHIPS, stride=4), :] for i in range(4)]
    top_bits, total_bits = got[2].astype(jnp.bfloat16), got[3].astype(jnp.bfloat16)
    for s in range(2):
        top = jnp.dot(top_bits, gather_step[s], preferred_element_type=jnp.float32)
        total = jnp.dot(total_bits, gather_step[s], preferred_element_type=jnp.float32)
        factor = jnp.exp(top - jnp.max(top, axis=0, keepdims=True))
        o_ref[s:s + 1, :] = jnp.sum(got[s] * factor, axis=0, keepdims=True) / jnp.sum(
            total * factor, axis=0, keepdims=True
        )

    gone = gath.at[0, pl.ds(0, CHIPS - 1)]
    pltpu.make_async_copy(gone, gone, gs_sem).wait()
    swap.wait_send()
    give.wait_send()
    gone = rbuf.at[pl.ds(0, CHIPS - 1)]
    pltpu.make_async_copy(gone, gone, rs_sem).wait()


def body(queries, keys, values, lengths):
    out = pl.pallas_call(
        kernel,
        out_shape=jax.ShapeDtypeStruct((2, 128), jnp.float32),
        in_specs=[
            pl.BlockSpec(memory_space=pltpu.HBM),
            pl.BlockSpec(memory_space=pltpu.HBM),
            pl.BlockSpec(memory_space=pltpu.HBM),
            pl.BlockSpec(memory_space=pltpu.HBM),
        ],
        out_specs=pl.BlockSpec(memory_space=pltpu.VMEM),
        scratch_shapes=[
            pltpu.VMEM((8, 32), jnp.bfloat16),
            pltpu.SMEM((4,), jnp.int32),
            pltpu.SemaphoreType.DMA((2,)),
            pltpu.VMEM((4, 256, 1024), jnp.bfloat16),
            pltpu.VMEM((4, 256, 1024), jnp.bfloat16),
            pltpu.VMEM((2, CHIPS, 2, 128), jnp.float32),
            pltpu.VMEM((2, CHIPS, 4, 128), jnp.float32),
            pltpu.VMEM((CHIPS, 4, 128), jnp.bfloat16),
            pltpu.VMEM((CHIPS, 4, 128), jnp.bfloat16),
            pltpu.VMEM((CHIPS, 4, 128), jnp.float32),
            pltpu.VMEM((CHIPS, 4, 128), jnp.float32),
            pltpu.SemaphoreType.DMA((8,)),
            pltpu.SemaphoreType.DMA,
            pltpu.SemaphoreType.DMA,
            pltpu.SemaphoreType.DMA((2,)),
            pltpu.SemaphoreType.DMA((2,)),
            pltpu.SemaphoreType.DMA,
            pltpu.SemaphoreType.DMA,
        ],
        compiler_params=pltpu.CompilerParams(
            collective_id=0, has_side_effects=True, vmem_limit_bytes=48 << 20
        ),
        cost_estimate=pl.CostEstimate(flops=67108864, bytes_accessed=4 << 20, transcendentals=131072),
    )(*[pltpu.with_memory_space_constraint(a, pltpu.HBM) for a in (queries.reshape(8, 32), lengths, keys, values)])
    return out.reshape(2, 4, 32)


def solution(mesh):
    in_specs = (
        P(None, None, ("inner", "outer")),
        P(None, ("inner", "outer"), None),
        P(None, ("inner", "outer"), None),
        P(),
    )
    out_specs = P(None, None, ("inner", "outer"))
    return jax.shard_map(body, mesh=mesh, in_specs=in_specs, out_specs=out_specs, check_vma=False)
```

```python
import functools

import jax
import jax.numpy as jnp
from jax import lax
from jax.experimental import pallas as pl
from jax.experimental.pallas import tpu as pltpu
from jax.sharding import PartitionSpec as P

HEAD_DIM = 128
NEGATIVE = -1e30
MESH = pl.DeviceIdType.MESH
NX, NZ, NY = 4, 8, 4
CHIPS = NX * NZ * NY


def lane_blocks(shape):
    return lax.broadcasted_iota(jnp.int32, shape, len(shape) - 1) // 32


def block_transpose(rows, block):
    odd = block % 2 == 1
    pairs = list(rows)
    for a in (0, 2):
        low, high = rows[a], rows[a + 1]
        pairs[a] = jnp.where(odd, pltpu.roll(high, 32, 1), low)
        pairs[a + 1] = jnp.where(odd, high, pltpu.roll(low, 96, 1))
    upper = block >= 2
    out = list(pairs)
    for a in (0, 1):
        low, high = pairs[a], pairs[a + 2]
        out[a] = jnp.where(upper, pltpu.roll(high, 64, 1), low)
        out[a + 2] = jnp.where(upper, high, pltpu.roll(low, 64, 1))
    return out


def kernel(
    q_hbm, len_hbm, k_hbm, v_hbm, o_ref,
    q_ref, len_ref, small_sem, keys, vals, gath, grows, sbuf, low, rbuf, wide, parts, load_sem, gs_sem, gr_sem, cs_sem, cr_sem, rs_sem, rr_sem,
):
    inner, outer = lax.axis_index("inner"), lax.axis_index("outer")
    x, z, y, core = inner // NZ, inner % NZ, outer // 2, outer % 2
    me = inner * NY + y
    other = 1 - core
    partner = (inner, y * 2 + other)

    q_load = pltpu.make_async_copy(q_hbm, q_ref, small_sem.at[0])
    q_load.start()
    len_load = pltpu.make_async_copy(len_hbm, len_ref, small_sem.at[1])
    len_load.start()
    loads = []
    for r in range(4):
        loads.append(pltpu.make_async_copy(k_hbm.at[r], keys.at[r], load_sem.at[r]))
        loads.append(pltpu.make_async_copy(v_hbm.at[r], vals.at[r], load_sem.at[4 + r]))

    xs = [lax.rem(x + i, NX) * NZ for i in range(NX)]
    zs = [lax.rem(z + i, NZ) for i in range(NZ)]
    ys = [lax.rem(y + i, NY) for i in range(NY)]
    peers = []
    for k in (4, 3, 5, 2, 6, 1, 7, 0):
        for i in (2, 1, 3, 0):
            for j in (2, 1, 3, 0):
                if i or j or k:
                    peers.append((xs[i] + zs[k], ys[j]))

    barrier = pltpu.get_barrier_semaphore()
    for pi, py in peers:
        pl.semaphore_signal(barrier, inc=1, device_id=(pi, py * 2 + core), device_id_type=MESH)
    pl.semaphore_signal(barrier, inc=1, device_id=partner, device_id_type=MESH)
    for load in loads:
        load.start()

    lane = lax.broadcasted_iota(jnp.int32, (1, 128), 1)
    spread = (lax.broadcasted_iota(jnp.int32, (32, 128), 0) == lax.broadcasted_iota(jnp.int32, (32, 128), 1) % 32)
    q_load.wait()
    len_load.wait()
    mine = jnp.dot(q_ref[...], spread.astype(jnp.bfloat16), preferred_element_type=jnp.float32)
    row = lax.broadcasted_iota(jnp.int32, (8, 128), 0)
    keep = row % 4 == lax.broadcasted_iota(jnp.int32, (8, 128), 1) // 32
    mine = jnp.where(keep, mine, 0.0)
    own = jnp.concatenate([jnp.sum(mine[4 * s:4 * s + 4], axis=0, keepdims=True) for s in range(2)], axis=0)
    gath[core, me] = own.astype(jnp.bfloat16)
    pl.semaphore_wait(barrier, CHIPS)

    for pi, py in peers:
        pltpu.make_async_remote_copy(
            src_ref=gath.at[core, me], dst_ref=gath.at[core, me], send_sem=gs_sem, recv_sem=gr_sem,
            device_id=(pi, py * 2 + core), device_id_type=MESH,
        ).start()
    all_but_one = gath.at[0, pl.ds(0, CHIPS - 1)]
    pltpu.make_async_copy(all_but_one, all_but_one, gr_sem).wait()
    swap = pltpu.make_async_remote_copy(
        src_ref=gath.at[core], dst_ref=gath.at[core], send_sem=cs_sem.at[0], recv_sem=cr_sem.at[0],
        device_id=partner, device_id_type=MESH,
    )
    swap.start()
    swap.wait_recv()
    for load in loads:
        load.wait()

    scale = 1.0 / HEAD_DIM**0.5
    block = lane_blocks((8, 128))
    first_half = lax.broadcasted_iota(jnp.int32, (8, 128), 1) % 32 < 16
    for c in range(2):
        grows[c] = gath.reshape(2, CHIPS * 2, 128)[c].astype(jnp.float32)
    srows = sbuf.reshape(2, CHIPS * 4, 128)
    fronts = []
    for g in range(8):
        pair = []
        for s in range(2):
            pieces = [grows[k % 2, pl.ds(g * 32 + (k // 2) * 2 + s, 8, stride=4), :] for k in range(4)]
            pair.append(block_transpose(pieces, block))
        fronts.append([jnp.concatenate([pair[0][r], pair[1][r]], axis=0).astype(jnp.bfloat16) for r in range(4)])

    position = (inner * 8 + outer) * 256 + lax.broadcasted_iota(jnp.int32, (256, 128), 0)
    step = lax.broadcasted_iota(jnp.int32, (256, 128), 1) // 8 % 2
    early = position - step
    blank = jnp.zeros((16, 128), jnp.bfloat16)
    results = [[None] * 4 for _ in range(8)]
    tops, totals = [], []
    scores = []
    for r in range(4):
        diagonal = jnp.concatenate(
            [jnp.concatenate([fronts[g][r] if a == g else blank for a in range(8)], axis=1) for g in range(8)], axis=0
        )
        scores.append(lax.dot_general(
            keys[r], diagonal, (((1,), (1,)), ((), ())), preferred_element_type=jnp.float32
        ))
    turned = []
    for r in range(4):
        score = jnp.where(early < len_ref[r], scores[r] * scale, NEGATIVE)
        top = jnp.max(score, axis=0, keepdims=True)
        weight = jnp.exp(score - jnp.maximum(top, 0.5 * NEGATIVE))
        tops.append(jnp.broadcast_to(top, (32, 128)))
        totals.append(jnp.broadcast_to(jnp.sum(weight, axis=0, keepdims=True), (32, 128)))
        turned.append(jnp.transpose(weight).astype(jnp.bfloat16))
    for r in range(4):
        for a in range(4):
            part = jnp.dot(
                turned[r][32 * a:32 * a + 32], vals[r, :, 256 * a:256 * a + 256], preferred_element_type=jnp.float32
            )
            results[2 * a][r] = part[:16, :128]
            results[2 * a + 1][r] = part[16:, 128:]
    top_cols = jnp.transpose(jnp.concatenate(tops, axis=0))
    total_cols = jnp.transpose(jnp.concatenate(totals, axis=0))
    for g in range(8):
        top_row = jnp.where(first_half, top_cols[16 * g:16 * g + 8], top_cols[16 * g + 8:16 * g + 16])
        total_row = jnp.where(first_half, total_cols[16 * g:16 * g + 8], total_cols[16 * g + 8:16 * g + 16])
        backs = [block_transpose([results[g][r][8 * s:8 * s + 8] for r in range(4)], block) for s in range(2)]
        for k in range(4):
            at = g * 64 + (k // 2) * 4
            for i, value in enumerate((backs[0][k], backs[1][k], top_row, total_row)):
                srows[k % 2, pl.ds(at + i, 8, stride=8), :] = value

    give = pltpu.make_async_remote_copy(
        src_ref=sbuf.at[other], dst_ref=parts, send_sem=cs_sem.at[1], recv_sem=cr_sem.at[1],
        device_id=partner, device_id_type=MESH,
    )
    give.start()
    give.wait_recv()

    tall = lax.broadcasted_iota(jnp.int32, (CHIPS, 128), 1)
    half = tall % 32 < 16

    def widen(v, half):
        return jnp.where(half, v, pltpu.roll(v, 16, 1)), jnp.where(half, pltpu.roll(v, 112, 1), v)

    def split(v):
        high = v.astype(jnp.bfloat16).astype(jnp.float32)
        rest = v - high
        middle = rest.astype(jnp.bfloat16).astype(jnp.float32)
        slot = tall % 16 // 4
        return jnp.where(slot == 0, high, jnp.where(slot == 1, middle, jnp.where(slot == 2, rest - middle, 0.0)))

    prows = parts.reshape(CHIPS * 4, 128)
    mine = [srows[core, pl.ds(i, CHIPS, stride=4), :] for i in range(4)]
    theirs = [prows[pl.ds(i, CHIPS, stride=4), :] for i in range(4)]
    high = jnp.maximum(mine[2], theirs[2])
    fm, ft = jnp.exp(mine[2] - high), jnp.exp(theirs[2] - high)
    wm, wt = widen(fm, half), widen(ft, half)
    for s in range(2):
        srows[core, pl.ds(s, CHIPS, stride=4), :] = mine[s] * wm[s] + theirs[s] * wt[s]
    srows[core, pl.ds(2, CHIPS, stride=4), :] = split(high)
    srows[core, pl.ds(3, CHIPS, stride=4), :] = split(mine[3] * fm + theirs[3] * ft)
    low.reshape(CHIPS * 4, 128)[...] = srows[core].astype(jnp.bfloat16)

    for pi, py in peers:
        pltpu.make_async_remote_copy(
            src_ref=low.at[pi * NY + py], dst_ref=rbuf.at[me], send_sem=rs_sem, recv_sem=rr_sem,
            device_id=(pi, py * 2 + core), device_id_type=MESH,
        ).start()
    rbuf[me] = low[me]
    source = lax.broadcasted_iota(jnp.int32, (128, 128), 0)
    target = lax.broadcasted_iota(jnp.int32, (128, 128), 1)
    same = source // 32 == target // 32
    gather_step = [(same & (source // 16 % 2 == s) & (source % 4 == 0)).astype(jnp.bfloat16) for s in range(2)]
    all_but_one = rbuf.at[pl.ds(0, CHIPS - 1)]
    pltpu.make_async_copy(all_but_one, all_but_one, rr_sem).wait()

    wide.reshape(CHIPS * 4, 128)[...] = rbuf.reshape(CHIPS * 4, 128)[...].astype(jnp.float32)
    wrows = wide.reshape(CHIPS * 4, 128)
    got = [wrows[pl.ds(i, CHIPS, stride=4), :] for i in range(4)]
    top_bits, total_bits = got[2].astype(jnp.bfloat16), got[3].astype(jnp.bfloat16)
    for s in range(2):
        top = jnp.dot(top_bits, gather_step[s], preferred_element_type=jnp.float32)
        total = jnp.dot(total_bits, gather_step[s], preferred_element_type=jnp.float32)
        factor = jnp.exp(top - jnp.max(top, axis=0, keepdims=True))
        o_ref[s:s + 1, :] = jnp.sum(got[s] * factor, axis=0, keepdims=True) / jnp.sum(
            total * factor, axis=0, keepdims=True
        )

    gone = gath.at[0, pl.ds(0, CHIPS - 1)]
    pltpu.make_async_copy(gone, gone, gs_sem).wait()
    swap.wait_send()
    give.wait_send()
    gone = rbuf.at[pl.ds(0, CHIPS - 1)]
    pltpu.make_async_copy(gone, gone, rs_sem).wait()


def body(queries, keys, values, lengths):
    out = pl.pallas_call(
        kernel,
        out_shape=jax.ShapeDtypeStruct((2, 128), jnp.float32),
        in_specs=[
            pl.BlockSpec(memory_space=pltpu.HBM),
            pl.BlockSpec(memory_space=pltpu.HBM),
            pl.BlockSpec(memory_space=pltpu.HBM),
            pl.BlockSpec(memory_space=pltpu.HBM),
        ],
        out_specs=pl.BlockSpec(memory_space=pltpu.VMEM),
        scratch_shapes=[
            pltpu.VMEM((8, 32), jnp.bfloat16),
            pltpu.SMEM((4,), jnp.int32),
            pltpu.SemaphoreType.DMA((2,)),
            pltpu.VMEM((4, 256, 1024), jnp.bfloat16),
            pltpu.VMEM((4, 256, 1024), jnp.bfloat16),
            pltpu.VMEM((2, CHIPS, 2, 128), jnp.bfloat16),
            pltpu.VMEM((2, CHIPS * 2, 128), jnp.float32),
            pltpu.VMEM((2, CHIPS, 4, 128), jnp.float32),
            pltpu.VMEM((CHIPS, 4, 128), jnp.bfloat16),
            pltpu.VMEM((CHIPS, 4, 128), jnp.bfloat16),
            pltpu.VMEM((CHIPS, 4, 128), jnp.float32),
            pltpu.VMEM((CHIPS, 4, 128), jnp.float32),
            pltpu.SemaphoreType.DMA((8,)),
            pltpu.SemaphoreType.DMA,
            pltpu.SemaphoreType.DMA,
            pltpu.SemaphoreType.DMA((2,)),
            pltpu.SemaphoreType.DMA((2,)),
            pltpu.SemaphoreType.DMA,
            pltpu.SemaphoreType.DMA,
        ],
        compiler_params=pltpu.CompilerParams(
            collective_id=0, has_side_effects=True, vmem_limit_bytes=48 << 20
        ),
        cost_estimate=pl.CostEstimate(flops=67108864, bytes_accessed=4 << 20, transcendentals=131072),
    )(*[pltpu.with_memory_space_constraint(a, pltpu.HBM) for a in (queries.reshape(8, 32), lengths, keys, values)])
    return out.reshape(2, 4, 32)


def solution(mesh):
    in_specs = (
        P(None, None, ("inner", "outer")),
        P(None, ("inner", "outer"), None),
        P(None, ("inner", "outer"), None),
        P(),
    )
    out_specs = P(None, None, ("inner", "outer"))
    return jax.shard_map(body, mesh=mesh, in_specs=in_specs, out_specs=out_specs, check_vma=False)
```
